512 devices in a mesh: row: 16 (over y_lo, x, core), col: 32 (over y_hi, z).
Axes of the slice: x: 4, y: 8 (y_hi: 4, y_lo: 2; y = y_hi * 2 + y_lo), z: 8, core: 2. Of those that a mesh axis runs over, the one named last changes fastest.
Arguments:
- out_left: bfloat16 [512, 512, 128], P('row', 'col'), may hold values from -6 to 6
- out_right: bfloat16 [512, 512, 128], P('col', 'row'), may hold values from -6 to 6
- in_left: bfloat16 [512, 512, 128], P('col', 'row'), may hold values from -6 to 6
- in_right: bfloat16 [512, 512, 128], P('row', 'col'), may hold values from -6 to 6
Outputs:
- outgoing: bfloat16 [512, 512, 128], P('row', 'col')
- incoming: bfloat16 [512, 512, 128], P('row', 'col')
The draws below stay inside these ranges and needn't reach their ends.
All inputs are finite; a program needn't handle non-finite values.
Results may differ from the reference program's by a relative error of at most 0.001.
Values may be sent and summed in bfloat16 or wider, within the bound.
No kernel may reach another device: no remote copies, remote signals or barrier semaphores. Data moves between devices by JAX's collectives and lax.ppermute only.
A program may use at most 128 MiB of HBM per device.

```python
import math
import jax
import jax.numpy as jnp

C = 128
N = 512


def shard_levels(own_key, shape, cuts, low, high):
    def one(dim, shards_of):
        heights = jax.random.uniform(jax.random.fold_in(jax.random.fold_in(own_key, 6), dim), (shards_of,), jnp.float32, low / len(cuts), high / len(cuts))
        return jnp.repeat(jnp.exp(heights), shape[dim] // shards_of).reshape((-1,) + (1,) * (len(shape) - dim - 1))

    level = one(*cuts[0])
    for cut in cuts[1:]:
        level = level * one(*cut)
    return level


def noise(stream_key, dims, width, most, shards=(), held_as=jnp.bfloat16):
    values = jax.random.normal(stream_key, dims, jnp.float32) * width
    if len(shards) > 0:
        values = shard_levels(stream_key, dims, shards, -0.22, 0.18) * values
    return jnp.clip(values, min=-most, max=most).astype(held_as)


def setup_inputs(seed: int = 0) -> dict:
    arg_keys = jax.random.split(jax.random.key(seed), 5)
    out_left = noise(arg_keys[0], (N, N, C), 1.0, 6.0, ((0, 16), (1, 32)))
    out_right = noise(arg_keys[1], (N, N, C), 1.0, 6.0, ((0, 32), (1, 16)))
    in_left = noise(arg_keys[2], (N, N, C), 1.0, 6.0, ((0, 32), (1, 16)))
    in_right = noise(arg_keys[3], (N, N, C), 1.0, 6.0, ((0, 16), (1, 32)))
    return {"out_left": out_left, "out_right": out_right, "in_left": in_left, "in_right": in_right}


def reference(out_left, out_right, in_left, in_right):
    factor = 1.0 / math.sqrt(N)
    prod_out = jnp.einsum('ikc,jkc->ijc', out_left.astype(jnp.float32), out_right.astype(jnp.float32))
    prod_in = jnp.einsum('kic,kjc->ijc', in_left.astype(jnp.float32), in_right.astype(jnp.float32))
    return ((prod_out * factor).astype(jnp.bfloat16), (prod_in * factor).astype(jnp.bfloat16))
```

```python
import math

import jax
import jax.numpy as jnp
from jax import lax
from jax.sharding import Mesh, PartitionSpec as P

ROW = ("y_lo", "x", "core")
COL = ("y_hi", "z")
CHIPS = ("y_lo", "x", "y_hi", "z")


def body(out_left, out_right, in_left, in_right):
    left = jnp.stack([out_left, in_left.transpose(1, 0, 2)])
    right = jnp.stack([out_right.transpose(1, 0, 2), in_right])
    both = jnp.stack([left, right])
    sent = both.transpose(1, 4, 0, 2, 3).reshape(256, 8, 128)
    got = lax.all_to_all(sent, CHIPS, 0, 0, tiled=True)
    got = got.reshape(8, 32, 2, 32, 16).transpose(2, 0, 3, 1, 4).reshape(2, 256, 512)
    other = lax.all_gather(got[1].reshape(8, 32, 512), "core", axis=1, tiled=False)
    total = jnp.dot(got[0], other.reshape(512, 512), preferred_element_type=jnp.float32)
    factor = 1.0 / math.sqrt(512)
    result = (total * factor).astype(jnp.bfloat16)
    back = result.reshape(8, 32, 32, 16).transpose(0, 2, 1, 3).reshape(256, 4, 128)
    mine = lax.all_to_all(back, CHIPS, 0, 0, tiled=True)
    mine = mine.reshape(2, 128, 512).transpose(0, 2, 1).reshape(2, 32, 16, 128)
    return mine[0], mine[1]


def solution(mesh):
    fine = Mesh(mesh.devices.reshape(2, 4, 2, 4, 8), ROW + COL)
    in_specs = (P(ROW, COL, None), P(COL, ROW, None), P(COL, ROW, None), P(ROW, COL, None))
    out_specs = (P(ROW, COL, None), P(ROW, COL, None))
    return jax.shard_map(body, mesh=fine, in_specs=in_specs, out_specs=out_specs, check_vma=False)
```

```python
import math

import jax
import jax.numpy as jnp
from jax import lax
from jax.experimental import pallas as pl
from jax.experimental.pallas import tpu as pltpu
from jax.sharding import Mesh, PartitionSpec as P

ROW = ("y_lo", "x", "core")
COL = ("y_hi", "z")
CHIPS = ("y_lo", "x", "y_hi", "z")
FACTOR = 1.0 / math.sqrt(512)
VMEM_BYTES = 32 * 1024 * 1024


def call(kernel, shape, scratch, *args):
    return pl.pallas_call(
        kernel,
        out_shape=shape,
        in_specs=[pl.BlockSpec(memory_space=pltpu.VMEM)] * len(args),
        out_specs=jax.tree.map(lambda _: pl.BlockSpec(memory_space=pltpu.VMEM), shape),
        scratch_shapes=[pltpu.VMEM(s, jnp.float32) for s in scratch],
        compiler_params=pltpu.CompilerParams(vmem_limit_bytes=VMEM_BYTES),
    )(*args)


def flip(block):
    n = block.shape[1]
    eye = lax.broadcasted_iota(jnp.int32, (n, n), 0) == lax.broadcasted_iota(jnp.int32, (n, n), 1)
    eye = eye.astype(jnp.float32).astype(jnp.bfloat16)
    return lax.dot_general(eye, block, (((1,), (1,)), ((), ())), preferred_element_type=jnp.float32)


def swap(v):
    lane = lax.broadcasted_iota(jnp.int32, v[0].shape, 1)
    even, low = (lane // 32) % 2 == 0, lane < 64

    def pair(x, y, first, by):
        return (
            jnp.where(first, x, pltpu.roll(y, by, 1)),
            jnp.where(first, pltpu.roll(x, 128 - by, 1), y),
        )

    a0, a1 = pair(v[0], v[1], even, 32)
    a2, a3 = pair(v[2], v[3], even, 32)
    w0, w2 = pair(a0, a2, low, 64)
    w1, w3 = pair(a1, a3, low, 64)
    return w0, w1, w2, w3


def pack_kernel(out_left, out_right, in_left, in_right, sent, rows, held):
    for product, side, ref, a_first in (
        (0, 0, out_left, True),
        (0, 1, out_right, False),
        (1, 0, in_left, False),
        (1, 1, in_right, True),
    ):
        if a_first:
            rows[...] = ref[...].reshape(512, 128).astype(jnp.float32)
            block = jnp.concatenate([rows[pl.ds(b, 32, stride=16), :] for b in range(16)])
            block = block.astype(jnp.bfloat16)
        else:
            block = ref[...].reshape(512, 128)
        turned = flip(block)
        for q in range(4):
            held[pl.ds(product * 1024 + side * 4 + q, 128, stride=8), :] = turned[:, q * 128 : (q + 1) * 128]
    sent[...] = held[...].astype(jnp.bfloat16).reshape(256, 8, 128)


def pack(out_left, out_right, in_left, in_right):
    return call(
        pack_kernel,
        jax.ShapeDtypeStruct((256, 8, 128), jnp.bfloat16),
        [(512, 128), (2048, 128)],
        out_left, out_right, in_left, in_right,
    )


def wide(ref, parts):
    return jnp.concatenate(
        [ref[p * 512 : (p + 1) * 512, :].astype(jnp.bfloat16) for p in range(parts)], axis=1
    )


def multiply_kernel(got, right, back, got_f, right_f, lhs, rhs, out):
    got_f[...] = got[...].reshape(2048, 128).astype(jnp.float32)
    right_f[...] = right[...].astype(jnp.float32).reshape(2048, 128)
    for q in range(4):
        for half in range(2):
            v = [got_f[pl.ds((half * 4 + r) * 256 + q, 32, stride=8), :] for r in range(4)]
            for g, w in enumerate(swap(v)):
                lhs[pl.ds(half * 512 + q * 4 + g, 32, stride=16), :] = w
        for part in range(4):
            v = [
                right_f[pl.ds((r % 2) * 1024 + (part * 2 + r // 2) * 128 + q, 32, stride=4), :]
                for r in range(4)
            ]
            for g, w in enumerate(swap(v)):
                rhs[pl.ds(part * 512 + q * 4 + g, 32, stride=16), :] = w
    total = FACTOR * jnp.dot(wide(rhs, 4), wide(lhs, 2), preferred_element_type=jnp.float32)
    for half in range(2):
        out[half * 512 : (half + 1) * 512, :] = total[:, half * 128 : (half + 1) * 128]
    for q in range(4):
        for half in range(2):
            v = [out[pl.ds(half * 512 + q * 4 + g, 32, stride=16), :] for g in range(4)]
            for r, w in enumerate(swap(v)):
                got_f[pl.ds((half * 4 + r) * 128 + q, 32, stride=4), :] = w
    back[...] = got_f[:1024, :].reshape(256, 4, 128).astype(jnp.bfloat16)


def multiply(got, right):
    return call(
        multiply_kernel,
        jax.ShapeDtypeStruct((256, 4, 128), jnp.bfloat16),
        [(2048, 128), (2048, 128), (1024, 128), (2048, 128), (1024, 128)],
        got, right,
    )


def unpack_kernel(mine, outgoing, incoming, held, rows):
    held[...] = mine[...].astype(jnp.float32).reshape(1024, 128)
    for product, ref in ((0, outgoing), (1, incoming)):
        for q in range(4):
            turned = flip(held[pl.ds(product * 512 + q, 128, stride=4), :].astype(jnp.bfloat16))
            for g in range(4):
                rows[pl.ds(q * 4 + g, 32, stride=16), :] = turned[g * 32 : (g + 1) * 32, :]
        ref[...] = rows[...].astype(jnp.bfloat16).reshape(32, 16, 128)


def unpack(mine):
    return call(
        unpack_kernel,
        (jax.ShapeDtypeStruct((32, 16, 128), jnp.bfloat16),) * 2,
        [(1024, 128), (512, 128)],
        mine,
    )


def body(out_left, out_right, in_left, in_right):
    got = lax.all_to_all(pack(out_left, out_right, in_left, in_right), CHIPS, 0, 0, tiled=True)
    right = lax.all_gather(got[:, 4:, :], "core", axis=0, tiled=False)
    back = multiply(got, right)
    return unpack(lax.all_to_all(back, CHIPS, 0, 0, tiled=True))


def solution(mesh):
    fine = Mesh(mesh.devices.reshape(2, 4, 2, 4, 8), ROW + COL)
    in_specs = (P(ROW, COL, None), P(COL, ROW, None), P(COL, ROW, None), P(ROW, COL, None))
    out_specs = (P(ROW, COL, None), P(ROW, COL, None))
    return jax.shard_map(body, mesh=fine, in_specs=in_specs, out_specs=out_specs, check_vma=False)
```

```python
import math

import jax
import jax.numpy as jnp
from jax import lax
from jax.experimental import pallas as pl
from jax.experimental.pallas import tpu as pltpu
from jax.sharding import Mesh, PartitionSpec as P

ROW = ("y_lo", "x", "core")
COL = ("y_hi", "z")
CHIPS = ("y_lo", "x", "y_hi", "z")
FACTOR = 1.0 / math.sqrt(512)
MIB = 1024 * 1024


def call(kernel, shape, scratch, *args, space=pltpu.VMEM, out_space=pltpu.VMEM, limit=32):
    return pl.pallas_call(
        kernel,
        out_shape=shape,
        in_specs=[pl.BlockSpec(memory_space=space)] * len(args),
        out_specs=jax.tree.map(lambda _: pl.BlockSpec(memory_space=out_space), shape),
        scratch_shapes=scratch,
        compiler_params=pltpu.CompilerParams(vmem_limit_bytes=limit * MIB),
    )(*args)


def f32(rows):
    return pltpu.VMEM((rows, 128), jnp.float32)


def flip(block):
    n = block.shape[1]
    eye = lax.broadcasted_iota(jnp.int32, (n, n), 0) == lax.broadcasted_iota(jnp.int32, (n, n), 1)
    eye = eye.astype(jnp.float32).astype(jnp.bfloat16)
    return lax.dot_general(eye, block, (((1,), (1,)), ((), ())), preferred_element_type=jnp.float32)


def swap(v):
    lane = lax.broadcasted_iota(jnp.int32, v[0].shape, 1)
    even, low = (lane // 32) % 2 == 0, lane < 64

    def pair(x, y, first, by):
        return (
            jnp.where(first, x, pltpu.roll(y, by, 1)),
            jnp.where(first, pltpu.roll(x, 128 - by, 1), y),
        )

    a0, a1 = pair(v[0], v[1], even, 32)
    a2, a3 = pair(v[2], v[3], even, 32)
    w0, w2 = pair(a0, a2, low, 64)
    w1, w3 = pair(a1, a3, low, 64)
    return w0, w1, w2, w3


def pack_kernel(blocks, sent, rows, held):
    for n, product, side, a_first in ((0, 0, 0, True), (1, 0, 1, False), (2, 1, 0, False), (3, 1, 1, True)):
        block = blocks[n]
        if a_first:
            rows[...] = block.astype(jnp.float32)
            block = jnp.concatenate([rows[pl.ds(b, 32, stride=16), :] for b in range(16)])
            block = block.astype(jnp.bfloat16)
        turned = flip(block)
        for q in range(4):
            held[pl.ds(product * 1024 + side * 4 + q, 128, stride=8), :] = turned[:, q * 128 : (q + 1) * 128]
    sent[...] = held[...].astype(jnp.bfloat16).reshape(256, 8, 128)


def pack(*blocks):
    return call(
        pack_kernel,
        jax.ShapeDtypeStruct((256, 8, 128), jnp.bfloat16),
        [f32(512), f32(2048)],
        jnp.stack([block.reshape(512, 128) for block in blocks]),
    )


def sort_kernel(got, left, right, got_f, sides):
    got_f[...] = got[...].astype(jnp.float32).reshape(2048, 128)
    for side, ref in ((1, right), (0, left)):
        for half in range(2):
            for q in range(4):
                v = [got_f[pl.ds((half * 4 + r) * 256 + side * 4 + q, 32, stride=8), :] for r in range(4)]
                for g, w in enumerate(swap(v)):
                    sides[pl.ds((side * 2 + half) * 512 + q * 4 + g, 32, stride=16), :] = w
            first = (side * 2 + half) * 512
            ref[:, half * 128 : (half + 1) * 128] = sides[first : first + 512, :].astype(jnp.bfloat16)


def sort(got):
    return call(
        sort_kernel,
        (jax.ShapeDtypeStruct((512, 256), jnp.bfloat16),) * 2,
        [f32(2048), f32(2048)],
        got,
    )


def multiply_kernel(left, right, back, out, held):
    total = None
    for core in range(2):
        lhs = jnp.concatenate([left[(2 * r + core) * 32 : (2 * r + core + 1) * 32, :] for r in range(8)])
        term = jnp.dot(right[core], lhs, preferred_element_type=jnp.float32)
        total = term if total is None else total + term
    total = total * FACTOR
    for half in range(2):
        out[half * 512 : (half + 1) * 512, :] = total[:, half * 128 : (half + 1) * 128]
        for q in range(4):
            v = [out[pl.ds(half * 512 + q * 4 + g, 32, stride=16), :] for g in range(4)]
            for r, w in enumerate(swap(v)):
                held[pl.ds((half * 4 + r) * 128 + q, 32, stride=4), :] = w
    back[...] = held[...].reshape(256, 4, 128).astype(jnp.bfloat16)


def multiply(left, right):
    return call(
        multiply_kernel,
        jax.ShapeDtypeStruct((256, 4, 128), jnp.bfloat16),
        [f32(1024), f32(1024)],
        left, right,
    )


def unpack_kernel(mine, outgoing, incoming, held, rows, done, sems):
    held[...] = mine[...].astype(jnp.float32).reshape(1024, 128)
    copies = []
    for product, ref in ((0, outgoing), (1, incoming)):
        for q in range(4):
            turned = flip(held[pl.ds(product * 512 + q, 128, stride=4), :].astype(jnp.bfloat16))
            for g in range(4):
                rows[pl.ds(product * 512 + q * 4 + g, 32, stride=16), :] = turned[g * 32 : (g + 1) * 32, :]
        block = rows[product * 512 : (product + 1) * 512, :].astype(jnp.bfloat16)
        done[product] = block.reshape(32, 16, 128)
        copies.append(pltpu.make_async_copy(done.at[product], ref, sems.at[product]))
        copies[-1].start()
    for copy in copies:
        copy.wait()


def unpack(mine):
    return call(
        unpack_kernel,
        (jax.ShapeDtypeStruct((32, 16, 128), jnp.bfloat16),) * 2,
        [f32(1024), f32(1024), pltpu.VMEM((2, 32, 16, 128), jnp.bfloat16), pltpu.SemaphoreType.DMA((2,))],
        mine, out_space=pltpu.HBM,
    )


def body(out_left, out_right, in_left, in_right):
    got = lax.all_to_all(pack(out_left, out_right, in_left, in_right), CHIPS, 0, 0, tiled=True)
    left, right = sort(got)
    both = lax.all_gather(right, "core", axis=0, tiled=False)
    back = multiply(left, both)
    return unpack(lax.all_to_all(back, CHIPS, 0, 0, tiled=True))


def solution(mesh):
    fine = Mesh(mesh.devices.reshape(2, 4, 2, 4, 8), ROW + COL)
    in_specs = (P(ROW, COL, None), P(COL, ROW, None), P(COL, ROW, None), P(ROW, COL, None))
    out_specs = (P(ROW, COL, None), P(ROW, COL, None))
    return jax.shard_map(body, mesh=fine, in_specs=in_specs, out_specs=out_specs, check_vma=False)
```

```python
import math

import jax
import jax.numpy as jnp
from jax import lax
from jax.experimental import pallas as pl
from jax.experimental.pallas import tpu as pltpu
from jax.sharding import Mesh, PartitionSpec as P

ROW = ("y_lo", "x", "core")
COL = ("y_hi", "z")
CHIPS = ("y_lo", "x", "y_hi", "z")
STEP = {"y_lo": 128, "x": 32, "z": 1}
FACTOR = 1.0 / math.sqrt(512)
MIB = 1024 * 1024


def call(kernel, shape, scratch, *args, space=pltpu.VMEM, out_space=pltpu.VMEM, limit=32):
    return pl.pallas_call(
        kernel,
        out_shape=shape,
        in_specs=[pl.BlockSpec(memory_space=space)] * len(args),
        out_specs=jax.tree.map(lambda _: pl.BlockSpec(memory_space=out_space), shape),
        scratch_shapes=scratch,
        compiler_params=pltpu.CompilerParams(vmem_limit_bytes=limit * MIB),
    )(*args)


def f32(rows):
    return pltpu.VMEM((rows, 128), jnp.float32)


def flip(block):
    n = block.shape[1]
    eye = lax.broadcasted_iota(jnp.int32, (n, n), 0) == lax.broadcasted_iota(jnp.int32, (n, n), 1)
    eye = eye.astype(jnp.float32).astype(jnp.bfloat16)
    return lax.dot_general(eye, block, (((1,), (1,)), ((), ())), preferred_element_type=jnp.float32)


def swap(v):
    lane = lax.broadcasted_iota(jnp.int32, v[0].shape, 1)
    even, low = (lane // 32) % 2 == 0, lane < 64

    def pair(x, y, first, by):
        return (
            jnp.where(first, x, pltpu.roll(y, by, 1)),
            jnp.where(first, pltpu.roll(x, 128 - by, 1), y),
        )

    a0, a1 = pair(v[0], v[1], even, 32)
    a2, a3 = pair(v[2], v[3], even, 32)
    w0, w2 = pair(a0, a2, low, 64)
    w1, w3 = pair(a1, a3, low, 64)
    return w0, w1, w2, w3


def pack_kernel(blocks, sent, rows, held):
    for n, product, side, a_first in ((0, 0, 0, True), (1, 0, 1, False), (2, 1, 0, False), (3, 1, 1, True)):
        block = blocks[n]
        if a_first:
            rows[...] = block.astype(jnp.float32)
            block = jnp.concatenate([rows[pl.ds(b, 32, stride=16), :] for b in range(16)])
            block = block.astype(jnp.bfloat16)
        turned = flip(block)
        for q in range(4):
            held[pl.ds(product * 1024 + side * 4 + q, 128, stride=8), :] = turned[:, q * 128 : (q + 1) * 128]
    sent[...] = held[...].astype(jnp.bfloat16).reshape(256, 8, 128)


def pack(*blocks):
    return call(
        pack_kernel,
        jax.ShapeDtypeStruct((256, 8, 128), jnp.bfloat16),
        [f32(512), f32(2048)],
        jnp.stack([block.reshape(512, 128) for block in blocks]),
    )


def chip_row(half, r):
    return half * STEP["y_lo"] + r * STEP["x"]


def sort_kernel(got, left, right, got_f, sorted_f):
    got_f[...] = got[...].astype(jnp.float32).reshape(2048, 128)
    for side in (1, 0):
        for half in range(2):
            lanes = slice(half * 128, (half + 1) * 128)
            for q in range(4):
                v = [got_f[pl.ds(chip_row(half, r) * 8 + side * 4 + q, 32, stride=STEP["z"] * 8), :] for r in range(4)]
                for g, w in enumerate(swap(v)):
                    b = q * 4 + g
                    if side == 1:
                        right[b * 32 : (b + 1) * 32, lanes] = w.astype(jnp.bfloat16)
                    else:
                        sorted_f[pl.ds(half * 512 + b, 32, stride=16), :] = w
            if side == 0:
                left[:, lanes] = sorted_f[half * 512 : (half + 1) * 512, :].astype(jnp.bfloat16)


def sort(got):
    return call(
        sort_kernel,
        (jax.ShapeDtypeStruct((512, 256), jnp.bfloat16),) * 2,
        [f32(2048), f32(1024)],
        got,
    )


def multiply_kernel(left, right, back, held):
    total = None
    for core in range(2):
        lhs = jnp.concatenate([left[(2 * r + core) * 32 : (2 * r + core + 1) * 32, :] for r in range(8)])
        term = jnp.dot(right[core], lhs, preferred_element_type=jnp.float32)
        total = term if total is None else total + term
    total = total * FACTOR
    for half in range(2):
        for q in range(4):
            v = [total[(q * 4 + g) * 32 : (q * 4 + g + 1) * 32, half * 128 : (half + 1) * 128] for g in range(4)]
            for r, w in enumerate(swap(v)):
                held[pl.ds(chip_row(half, r) * 4 + q, 32, stride=STEP["z"] * 4), :] = w
    back[...] = held[...].reshape(256, 4, 128).astype(jnp.bfloat16)


def multiply(left, right):
    return call(
        multiply_kernel,
        jax.ShapeDtypeStruct((256, 4, 128), jnp.bfloat16),
        [f32(1024)],
        left, right,
    )


def unpack_kernel(mine, outgoing, incoming, held, rows, done, sems):
    held[...] = mine[...].astype(jnp.float32).reshape(1024, 128)
    copies = []
    for product, ref in ((0, outgoing), (1, incoming)):
        for q in range(4):
            turned = flip(held[pl.ds(product * 512 + q, 128, stride=4), :].astype(jnp.bfloat16))
            for g in range(4):
                rows[pl.ds(product * 512 + q * 4 + g, 32, stride=16), :] = turned[g * 32 : (g + 1) * 32, :]
        block = rows[product * 512 : (product + 1) * 512, :].astype(jnp.bfloat16)
        done[product] = block.reshape(32, 16, 128)
        copies.append(pltpu.make_async_copy(done.at[product], ref, sems.at[product]))
        copies[-1].start()
    for copy in copies:
        copy.wait()


def unpack(mine):
    return call(
        unpack_kernel,
        (jax.ShapeDtypeStruct((32, 16, 128), jnp.bfloat16),) * 2,
        [f32(1024), f32(1024), pltpu.VMEM((2, 32, 16, 128), jnp.bfloat16), pltpu.SemaphoreType.DMA((2,))],
        mine, out_space=pltpu.HBM,
    )


def body(out_left, out_right, in_left, in_right):
    got = lax.all_to_all(pack(out_left, out_right, in_left, in_right), CHIPS, 0, 0, tiled=True)
    left, right = sort(got)
    both = lax.all_gather(right, "core", axis=0, tiled=False)
    back = multiply(left, both)
    return unpack(lax.all_to_all(back, CHIPS, 0, 0, tiled=True))


def solution(mesh):
    fine = Mesh(mesh.devices.reshape(2, 4, 2, 4, 8), ROW + COL)
    in_specs = (P(ROW, COL, None), P(COL, ROW, None), P(COL, ROW, None), P(ROW, COL, None))
    out_specs = (P(ROW, COL, None), P(ROW, COL, None))
    return jax.shard_map(body, mesh=fine, in_specs=in_specs, out_specs=out_specs, check_vma=False)
```

```python
import math

import jax
import jax.numpy as jnp
from jax import lax
from jax.experimental import pallas as pl
from jax.experimental.pallas import tpu as pltpu
from jax.sharding import Mesh, PartitionSpec as P

ROW = ("y_lo", "x", "core")
COL = ("y_hi", "z")
CHIPS = ("y_lo", "x", "y_hi", "z")
STEP = {"y_lo": 128, "x": 32, "z": 1}
FACTOR = 1.0 / math.sqrt(512)
MIB = 1024 * 1024


def call(kernel, shape, scratch, *args, space=pltpu.VMEM, out_space=pltpu.VMEM, limit=32):
    return pl.pallas_call(
        kernel,
        out_shape=shape,
        in_specs=[pl.BlockSpec(memory_space=space)] * len(args),
        out_specs=jax.tree.map(lambda _: pl.BlockSpec(memory_space=out_space), shape),
        scratch_shapes=scratch,
        compiler_params=pltpu.CompilerParams(vmem_limit_bytes=limit * MIB),
    )(*args)


def f32(rows):
    return pltpu.VMEM((rows, 128), jnp.float32)


def flip(block):
    n = block.shape[1]
    eye = lax.broadcasted_iota(jnp.int32, (n, n), 0) == lax.broadcasted_iota(jnp.int32, (n, n), 1)
    eye = eye.astype(jnp.float32).astype(jnp.bfloat16)
    return lax.dot_general(eye, block, (((1,), (1,)), ((), ())), preferred_element_type=jnp.float32)


def swap(v):
    lane = lax.broadcasted_iota(jnp.int32, v[0].shape, 1)
    even, low = (lane // 32) % 2 == 0, lane < 64
    middle = (lane >= 32) & (lane < 96)

    def pair(x, y):
        moved = pltpu.roll(jnp.where(even, y, x), 32, 1)
        return jnp.where(even, x, moved), jnp.where(even, moved, y)

    a0, a1 = pair(v[0], v[1])
    a2, a3 = pair(v[2], v[3])
    moved = pltpu.roll(jnp.where(low, a2, a0), 64, 1)
    w0, w2 = jnp.where(low, a0, moved), jnp.where(low, moved, a2)
    moved, kept = pltpu.roll(jnp.where(low, a3, a1), 64, 1), jnp.where(low, a1, a3)
    w1, w3 = jnp.where(middle, kept, moved), jnp.where(middle, moved, kept)
    return w0, w1, w2, w3


def pack_kernel(blocks, sent, rows, held):
    for n, product, side, a_first in ((0, 0, 0, True), (1, 0, 1, False), (2, 1, 0, False), (3, 1, 1, True)):
        block = blocks[n]
        if a_first:
            rows[...] = block.astype(jnp.float32)
            block = jnp.concatenate([rows[pl.ds(b, 32, stride=16), :] for b in range(16)])
            block = block.astype(jnp.bfloat16)
        turned = flip(block)
        for q in range(4):
            held[pl.ds(product * 1024 + side * 4 + q, 128, stride=8), :] = turned[:, q * 128 : (q + 1) * 128]
    sent[...] = held[...].astype(jnp.bfloat16).reshape(256, 8, 128)


def pack(*blocks):
    return call(
        pack_kernel,
        jax.ShapeDtypeStruct((256, 8, 128), jnp.bfloat16),
        [f32(512), f32(2048)],
        jnp.stack([block.reshape(512, 128) for block in blocks]),
    )


def chip_row(half, r):
    return half * STEP["y_lo"] + r * STEP["x"]


def sort_kernel(got, left, right, got_f, sorted_f):
    got_f[...] = got[...].astype(jnp.float32).reshape(2048, 128)
    for side in (1, 0):
        for half in range(2):
            lanes = slice(half * 128, (half + 1) * 128)
            for q in range(4):
                v = [got_f[pl.ds(chip_row(half, r) * 8 + side * 4 + q, 32, stride=STEP["z"] * 8), :] for r in range(4)]
                for g, w in enumerate(swap(v)):
                    b = q * 4 + g
                    if side == 1:
                        right[b * 32 : (b + 1) * 32, lanes] = w.astype(jnp.bfloat16)
                    else:
                        sorted_f[pl.ds(half * 512 + b, 32, stride=16), :] = w
            if side == 0:
                left[:, lanes] = sorted_f[half * 512 : (half + 1) * 512, :].astype(jnp.bfloat16)


def sort(got):
    return call(
        sort_kernel,
        (jax.ShapeDtypeStruct((512, 256), jnp.bfloat16),) * 2,
        [f32(2048), f32(1024)],
        got,
    )


def multiply_kernel(left, right, back, held):
    total = None
    for core in range(2):
        lhs = jnp.concatenate([left[(2 * r + core) * 32 : (2 * r + core + 1) * 32, :] for r in range(8)])
        term = jnp.dot(right[core], lhs, preferred_element_type=jnp.float32)
        total = term if total is None else total + term
    total = total * FACTOR
    for half in range(2):
        for q in range(4):
            v = [total[(q * 4 + g) * 32 : (q * 4 + g + 1) * 32, half * 128 : (half + 1) * 128] for g in range(4)]
            for r, w in enumerate(swap(v)):
                held[pl.ds(chip_row(half, r) * 4 + q, 32, stride=STEP["z"] * 4), :] = w
    back[...] = held[...].reshape(256, 4, 128).astype(jnp.bfloat16)


def multiply(left, right):
    return call(
        multiply_kernel,
        jax.ShapeDtypeStruct((256, 4, 128), jnp.bfloat16),
        [f32(1024)],
        left, right,
    )


def unpack_kernel(mine, outgoing, incoming, held, rows, done, sems):
    held[...] = mine[...].astype(jnp.float32).reshape(1024, 128)
    copies = []
    for product, ref in ((0, outgoing), (1, incoming)):
        for q in range(4):
            turned = flip(held[pl.ds(product * 512 + q, 128, stride=4), :].astype(jnp.bfloat16))
            for g in range(4):
                rows[pl.ds(product * 512 + q * 4 + g, 32, stride=16), :] = turned[g * 32 : (g + 1) * 32, :]
        block = rows[product * 512 : (product + 1) * 512, :].astype(jnp.bfloat16)
        done[product] = block.reshape(32, 16, 128)
        copies.append(pltpu.make_async_copy(done.at[product], ref, sems.at[product]))
        copies[-1].start()
    for copy in copies:
        copy.wait()


def unpack(mine):
    return call(
        unpack_kernel,
        (jax.ShapeDtypeStruct((32, 16, 128), jnp.bfloat16),) * 2,
        [f32(1024), f32(1024), pltpu.VMEM((2, 32, 16, 128), jnp.bfloat16), pltpu.SemaphoreType.DMA((2,))],
        mine, out_space=pltpu.HBM,
    )


def body(out_left, out_right, in_left, in_right):
    got = lax.all_to_all(pack(out_left, out_right, in_left, in_right), CHIPS, 0, 0, tiled=True)
    left, right = sort(got)
    both = lax.all_gather(right, "core", axis=0, tiled=False)
    back = multiply(left, both)
    return unpack(lax.all_to_all(back, CHIPS, 0, 0, tiled=True))


def solution(mesh):
    fine = Mesh(mesh.devices.reshape(2, 4, 2, 4, 8), ROW + COL)
    in_specs = (P(ROW, COL, None), P(COL, ROW, None), P(COL, ROW, None), P(ROW, COL, None))
    out_specs = (P(ROW, COL, None), P(ROW, COL, None))
    return jax.shard_map(body, mesh=fine, in_specs=in_specs, out_specs=out_specs, check_vma=False)
```

```python
import math

import jax
import jax.numpy as jnp
from jax import lax
from jax.experimental import pallas as pl
from jax.experimental.pallas import tpu as pltpu
from jax.sharding import Mesh, PartitionSpec as P

ROW = ("y_lo", "x", "core")
COL = ("y_hi", "z")
CHIPS = ("y_hi", "y_lo", "z", "x")
STEP = {"y_hi": 64, "y_lo": 32, "z": 4, "x": 1}
FACTOR = 1.0 / math.sqrt(512)
MIB = 1024 * 1024


def call(kernel, shape, scratch, *args, space=pltpu.VMEM, out_space=pltpu.VMEM, limit=32):
    return pl.pallas_call(
        kernel,
        out_shape=shape,
        in_specs=[pl.BlockSpec(memory_space=space)] * len(args),
        out_specs=jax.tree.map(lambda _: pl.BlockSpec(memory_space=out_space), shape),
        scratch_shapes=scratch,
        compiler_params=pltpu.CompilerParams(vmem_limit_bytes=limit * MIB),
    )(*args)


def f32(rows):
    return pltpu.VMEM((rows, 128), jnp.float32)


def flip(block):
    n = block.shape[1]
    eye = lax.broadcasted_iota(jnp.int32, (n, n), 0) == lax.broadcasted_iota(jnp.int32, (n, n), 1)
    eye = eye.astype(jnp.float32).astype(jnp.bfloat16)
    return lax.dot_general(eye, block, (((1,), (1,)), ((), ())), preferred_element_type=jnp.float32)


def swap(v):
    lane = lax.broadcasted_iota(jnp.int32, v[0].shape, 1)
    even, low = (lane // 32) % 2 == 0, lane < 64
    middle = (lane >= 32) & (lane < 96)

    def pair(x, y):
        moved = pltpu.roll(jnp.where(even, y, x), 32, 1)
        return jnp.where(even, x, moved), jnp.where(even, moved, y)

    a0, a1 = pair(v[0], v[1])
    a2, a3 = pair(v[2], v[3])
    moved = pltpu.roll(jnp.where(low, a2, a0), 64, 1)
    w0, w2 = jnp.where(low, a0, moved), jnp.where(low, moved, a2)
    moved, kept = pltpu.roll(jnp.where(low, a3, a1), 64, 1), jnp.where(low, a1, a3)
    w1, w3 = jnp.where(middle, kept, moved), jnp.where(middle, moved, kept)
    return w0, w1, w2, w3


def pack_kernel(blocks, sent, rows, held):
    for n, product, side, a_first in ((0, 0, 0, True), (1, 0, 1, False), (2, 1, 0, False), (3, 1, 1, True)):
        block = blocks[n]
        if a_first:
            rows[...] = block.astype(jnp.float32)
            block = jnp.concatenate([rows[pl.ds(b, 32, stride=16), :] for b in range(16)])
            block = block.astype(jnp.bfloat16)
        turned = flip(block)
        for q in range(4):
            held[pl.ds(product * 1024 + side * 4 + q, 128, stride=8), :] = turned[:, q * 128 : (q + 1) * 128]
    sent[...] = held[...].astype(jnp.bfloat16).reshape(256, 8, 128)


def pack(*blocks):
    return call(
        pack_kernel,
        jax.ShapeDtypeStruct((256, 8, 128), jnp.bfloat16),
        [f32(512), f32(2048)],
        jnp.stack([block.reshape(512, 128) for block in blocks]),
    )


def chip_rows(half, r, y, height, row):
    first = half * STEP["y_lo"] + r * STEP["x"] + y * STEP["y_hi"]
    return pl.ds(first * height + row, 8, stride=STEP["z"] * height)


def sort_kernel(got, left, right, got_f, sorted_f):
    got_f[...] = got[...].astype(jnp.float32).reshape(2048, 128)
    for side in (1, 0):
        for half in range(2):
            lanes = slice(half * 128, (half + 1) * 128)
            for q in range(4):
                v = [
                    jnp.concatenate([got_f[chip_rows(half, r, y, 8, side * 4 + q), :] for y in range(4)])
                    for r in range(4)
                ]
                for g, w in enumerate(swap(v)):
                    b = q * 4 + g
                    if side == 1:
                        right[b * 32 : (b + 1) * 32, lanes] = w.astype(jnp.bfloat16)
                    else:
                        sorted_f[pl.ds(half * 512 + b, 32, stride=16), :] = w
            if side == 0:
                left[:, lanes] = sorted_f[half * 512 : (half + 1) * 512, :].astype(jnp.bfloat16)


def sort(got):
    return call(
        sort_kernel,
        (jax.ShapeDtypeStruct((512, 256), jnp.bfloat16),) * 2,
        [f32(2048), f32(1024)],
        got,
    )


def multiply_kernel(left, right, back, held):
    total = None
    for core in range(2):
        lhs = jnp.concatenate([left[(2 * r + core) * 32 : (2 * r + core + 1) * 32, :] for r in range(8)])
        term = jnp.dot(right[core], lhs, preferred_element_type=jnp.float32)
        total = term if total is None else total + term
    total = total * FACTOR
    for half in range(2):
        for q in range(4):
            v = [total[(q * 4 + g) * 32 : (q * 4 + g + 1) * 32, half * 128 : (half + 1) * 128] for g in range(4)]
            for r, w in enumerate(swap(v)):
                for y in range(4):
                    held[chip_rows(half, r, y, 4, q), :] = w[y * 8 : (y + 1) * 8, :]
    back[...] = held[...].reshape(256, 4, 128).astype(jnp.bfloat16)


def multiply(left, right):
    return call(
        multiply_kernel,
        jax.ShapeDtypeStruct((256, 4, 128), jnp.bfloat16),
        [f32(1024)],
        left, right,
    )


def unpack_kernel(mine, outgoing, incoming, held, rows, done, sems):
    held[...] = mine[...].astype(jnp.float32).reshape(1024, 128)
    copies = []
    for product, ref in ((0, outgoing), (1, incoming)):
        for q in range(4):
            turned = flip(held[pl.ds(product * 512 + q, 128, stride=4), :].astype(jnp.bfloat16))
            for g in range(4):
                rows[pl.ds(product * 512 + q * 4 + g, 32, stride=16), :] = turned[g * 32 : (g + 1) * 32, :]
        block = rows[product * 512 : (product + 1) * 512, :].astype(jnp.bfloat16)
        done[product] = block.reshape(32, 16, 128)
        copies.append(pltpu.make_async_copy(done.at[product], ref, sems.at[product]))
        copies[-1].start()
    for copy in copies:
        copy.wait()


def unpack(mine):
    return call(
        unpack_kernel,
        (jax.ShapeDtypeStruct((32, 16, 128), jnp.bfloat16),) * 2,
        [f32(1024), f32(1024), pltpu.VMEM((2, 32, 16, 128), jnp.bfloat16), pltpu.SemaphoreType.DMA((2,))],
        mine, out_space=pltpu.HBM,
    )


def body(out_left, out_right, in_left, in_right):
    got = lax.all_to_all(pack(out_left, out_right, in_left, in_right), CHIPS, 0, 0, tiled=True)
    left, right = sort(got)
    both = lax.all_gather(right, "core", axis=0, tiled=False)
    back = multiply(left, both)
    return unpack(lax.all_to_all(back, CHIPS, 0, 0, tiled=True))


def solution(mesh):
    fine = Mesh(mesh.devices.reshape(2, 4, 2, 4, 8), ROW + COL)
    in_specs = (P(ROW, COL, None), P(COL, ROW, None), P(COL, ROW, None), P(ROW, COL, None))
    out_specs = (P(ROW, COL, None), P(ROW, COL, None))
    return jax.shard_map(body, mesh=fine, in_specs=in_specs, out_specs=out_specs, check_vma=False)
```

```python
import math

import jax
import jax.numpy as jnp
from jax import lax
from jax.experimental import pallas as pl
from jax.experimental.pallas import tpu as pltpu
from jax.sharding import Mesh, PartitionSpec as P

ROW = ("y_lo", "x", "core")
COL = ("y_hi", "z")
CHIPS = ("y_hi", "y_lo", "z", "x")
STEP = {"y_hi": 64, "y_lo": 32, "z": 4, "x": 1}
FACTOR = 1.0 / math.sqrt(512)
MIB = 1024 * 1024


def call(kernel, shape, scratch, *args, space=pltpu.VMEM, out_space=pltpu.VMEM, limit=32):
    return pl.pallas_call(
        kernel,
        out_shape=shape,
        in_specs=[pl.BlockSpec(memory_space=space)] * len(args),
        out_specs=jax.tree.map(lambda _: pl.BlockSpec(memory_space=out_space), shape),
        scratch_shapes=scratch,
        compiler_params=pltpu.CompilerParams(vmem_limit_bytes=limit * MIB),
    )(*args)


def f32(rows):
    return pltpu.VMEM((rows, 128), jnp.float32)


def swap(v):
    lane = lax.broadcasted_iota(jnp.int32, v[0].shape, 1)
    even, low = (lane // 32) % 2 == 0, lane < 64
    middle = (lane >= 32) & (lane < 96)

    def pair(x, y):
        moved = pltpu.roll(jnp.where(even, y, x), 32, 1)
        return jnp.where(even, x, moved), jnp.where(even, moved, y)

    a0, a1 = pair(v[0], v[1])
    a2, a3 = pair(v[2], v[3])
    moved = pltpu.roll(jnp.where(low, a2, a0), 64, 1)
    w0, w2 = jnp.where(low, a0, moved), jnp.where(low, moved, a2)
    moved, kept = pltpu.roll(jnp.where(low, a3, a1), 64, 1), jnp.where(low, a1, a3)
    w1, w3 = jnp.where(middle, kept, moved), jnp.where(middle, moved, kept)
    return w0, w1, w2, w3


def pack_kernel(blocks, sent, rows, held):
    for n, product, side, a_first in ((0, 0, 0, True), (1, 0, 1, False), (2, 1, 0, False), (3, 1, 1, True)):
        block = blocks[n]
        if a_first:
            rows[...] = block.astype(jnp.float32)
            block = jnp.concatenate([rows[pl.ds(b, 32, stride=16), :] for b in range(16)])
            block = block.astype(jnp.bfloat16)
        turned = block.astype(jnp.float32).T
        for q in range(4):
            held[pl.ds(product * 1024 + side * 4 + q, 128, stride=8), :] = turned[:, q * 128 : (q + 1) * 128]
    sent[...] = held[...].astype(jnp.bfloat16).reshape(256, 8, 128)


def pack(*blocks):
    return call(
        pack_kernel,
        jax.ShapeDtypeStruct((256, 8, 128), jnp.bfloat16),
        [f32(512), f32(2048)],
        jnp.stack([block.reshape(512, 128) for block in blocks]),
    )


def chip_rows(half, r, y, q):
    first = half * STEP["y_lo"] + r * STEP["x"] + y * STEP["y_hi"]
    return pl.ds(first * 4 + q, 8, stride=STEP["z"] * 4)


def sort_kernel(got, left, right, got_f, sorted_f):
    tiles = got[...].astype(jnp.float32).reshape(64, 4, 8, 128)
    for r in range(4):
        got_f[r * 512 : (r + 1) * 512, :] = tiles[:, r].reshape(512, 128)
    for side in (1, 0):
        for half in range(2):
            lanes = slice(half * 128, (half + 1) * 128)
            for q in range(4):
                v = [
                    jnp.concatenate(
                        [got_f[pl.ds((r * 64 + y * 16 + half * 8) * 8 + side * 4 + q, 8, stride=8), :] for y in range(4)]
                    )
                    for r in range(4)
                ]
                for g, w in enumerate(swap(v)):
                    b = q * 4 + g
                    if side == 1:
                        right[b * 32 : (b + 1) * 32, lanes] = w.astype(jnp.bfloat16)
                    else:
                        sorted_f[pl.ds(half * 512 + b, 32, stride=16), :] = w
            if side == 0:
                left[:, lanes] = sorted_f[half * 512 : (half + 1) * 512, :].astype(jnp.bfloat16)


def sort(got):
    return call(
        sort_kernel,
        (jax.ShapeDtypeStruct((512, 256), jnp.bfloat16),) * 2,
        [f32(2048), f32(1024)],
        got,
    )


def multiply_kernel(left, right, back, held):
    total = None
    for core in range(2):
        lhs = jnp.concatenate([left[(2 * r + core) * 32 : (2 * r + core + 1) * 32, :] for r in range(8)])
        term = jnp.dot(right[core], lhs, preferred_element_type=jnp.float32)
        total = term if total is None else total + term
    total = total * FACTOR
    for half in range(2):
        for q in range(4):
            v = [total[(q * 4 + g) * 32 : (q * 4 + g + 1) * 32, half * 128 : (half + 1) * 128] for g in range(4)]
            for r, w in enumerate(swap(v)):
                for y in range(4):
                    held[chip_rows(half, r, y, q), :] = w[y * 8 : (y + 1) * 8, :]
    back[...] = held[...].reshape(256, 4, 128).astype(jnp.bfloat16)


def multiply(left, right):
    return call(
        multiply_kernel,
        jax.ShapeDtypeStruct((256, 4, 128), jnp.bfloat16),
        [f32(1024)],
        left, right,
    )


def unpack_kernel(mine, outgoing, incoming, held, rows, done, sems):
    held[...] = mine[...].astype(jnp.float32).reshape(1024, 128)
    copies = []
    for product, ref in ((0, outgoing), (1, incoming)):
        for q in range(4):
            turned = held[pl.ds(product * 512 + q, 128, stride=4), :].T
            for g in range(4):
                rows[pl.ds(product * 512 + q * 4 + g, 32, stride=16), :] = turned[g * 32 : (g + 1) * 32, :]
        block = rows[product * 512 : (product + 1) * 512, :].astype(jnp.bfloat16)
        done[product] = block.reshape(32, 16, 128)
        copies.append(pltpu.make_async_copy(done.at[product], ref, sems.at[product]))
        copies[-1].start()
    for copy in copies:
        copy.wait()


def unpack(mine):
    return call(
        unpack_kernel,
        (jax.ShapeDtypeStruct((32, 16, 128), jnp.bfloat16),) * 2,
        [f32(1024), f32(1024), pltpu.VMEM((2, 32, 16, 128), jnp.bfloat16), pltpu.SemaphoreType.DMA((2,))],
        mine, out_space=pltpu.HBM,
    )


def body(out_left, out_right, in_left, in_right):
    got = lax.all_to_all(pack(out_left, out_right, in_left, in_right), CHIPS, 0, 0, tiled=True)
    left, right = sort(got)
    both = lax.all_gather(right, "core", axis=0, tiled=False)
    back = multiply(left, both)
    return unpack(lax.all_to_all(back, CHIPS, 0, 0, tiled=True))


def solution(mesh):
    fine = Mesh(mesh.devices.reshape(2, 4, 2, 4, 8), ROW + COL)
    in_specs = (P(ROW, COL, None), P(COL, ROW, None), P(COL, ROW, None), P(ROW, COL, None))
    out_specs = (P(ROW, COL, None), P(ROW, COL, None))
    return jax.shard_map(body, mesh=fine, in_specs=in_specs, out_specs=out_specs, check_vma=False)
```

```python
import math

import jax
import jax.numpy as jnp
from jax import lax
from jax.experimental import pallas as pl
from jax.experimental.pallas import tpu as pltpu
from jax.sharding import Mesh, PartitionSpec as P

ROW = ("y_lo", "x", "core")
COL = ("y_hi", "z")
CHIPS = ("y_hi", "y_lo", "z", "x")
STEP = {"y_hi": 64, "y_lo": 32, "z": 4, "x": 1}
FACTOR = 1.0 / math.sqrt(512)
MIB = 1024 * 1024


def call(kernel, shape, scratch, *args, space=pltpu.VMEM, out_space=pltpu.VMEM, limit=32):
    return pl.pallas_call(
        kernel,
        out_shape=shape,
        in_specs=[pl.BlockSpec(memory_space=space)] * len(args),
        out_specs=jax.tree.map(lambda _: pl.BlockSpec(memory_space=out_space), shape),
        scratch_shapes=scratch,
        compiler_params=pltpu.CompilerParams(vmem_limit_bytes=limit * MIB),
    )(*args)


def f32(rows):
    return pltpu.VMEM((rows, 128), jnp.float32)


def swap(v):
    lane = lax.broadcasted_iota(jnp.int32, v[0].shape, 1)
    even, low = (lane // 32) % 2 == 0, lane < 64
    middle = (lane >= 32) & (lane < 96)

    def pair(x, y):
        moved = pltpu.roll(jnp.where(even, y, x), 32, 1)
        return jnp.where(even, x, moved), jnp.where(even, moved, y)

    a0, a1 = pair(v[0], v[1])
    a2, a3 = pair(v[2], v[3])
    moved = pltpu.roll(jnp.where(low, a2, a0), 64, 1)
    w0, w2 = jnp.where(low, a0, moved), jnp.where(low, moved, a2)
    moved, kept = pltpu.roll(jnp.where(low, a3, a1), 64, 1), jnp.where(low, a1, a3)
    w1, w3 = jnp.where(middle, kept, moved), jnp.where(middle, moved, kept)
    return w0, w1, w2, w3


def pack_kernel(blocks, sent, rows, held):
    for n, product, side, a_first in ((0, 0, 0, True), (1, 0, 1, False), (2, 1, 0, False), (3, 1, 1, True)):
        block = blocks[n]
        if a_first:
            rows[...] = block.astype(jnp.float32)
            block = jnp.concatenate([rows[pl.ds(b, 32, stride=16), :] for b in range(16)])
            block = block.astype(jnp.bfloat16)
        turned = block.astype(jnp.float32).T
        for q in range(4):
            held[pl.ds(product * 1024 + side * 4 + q, 128, stride=8), :] = turned[:, q * 128 : (q + 1) * 128]
    sent[...] = held[...].astype(jnp.bfloat16).reshape(256, 8, 128)


def pack(*blocks):
    return call(
        pack_kernel,
        jax.ShapeDtypeStruct((256, 8, 128), jnp.bfloat16),
        [f32(512), f32(2048)],
        jnp.concatenate([block.reshape(512, 128) for block in blocks]).reshape(4, 512, 128),
    )


def chip_rows(half, r, y, q):
    first = half * STEP["y_lo"] + r * STEP["x"] + y * STEP["y_hi"]
    return pl.ds(first * 4 + q, 8, stride=STEP["z"] * 4)


def sort_kernel(got, left, right, got_f, sorted_f):
    tiles = got[...].astype(jnp.float32).reshape(64, 4, 8, 128)
    for r in range(4):
        got_f[r * 512 : (r + 1) * 512, :] = tiles[:, r].reshape(512, 128)
    for side in (1, 0):
        for half in range(2):
            lanes = slice(half * 128, (half + 1) * 128)
            for q in range(4):
                v = [
                    jnp.concatenate(
                        [got_f[pl.ds((r * 64 + y * 16 + half * 8) * 8 + side * 4 + q, 8, stride=8), :] for y in range(4)]
                    )
                    for r in range(4)
                ]
                for g, w in enumerate(swap(v)):
                    b = q * 4 + g
                    if side == 1:
                        right[b * 32 : (b + 1) * 32, lanes] = w.astype(jnp.bfloat16)
                    else:
                        sorted_f[pl.ds(half * 512 + b, 32, stride=16), :] = w
            if side == 0:
                left[:, lanes] = sorted_f[half * 512 : (half + 1) * 512, :].astype(jnp.bfloat16)


def sort(got):
    return call(
        sort_kernel,
        (jax.ShapeDtypeStruct((512, 256), jnp.bfloat16),) * 2,
        [f32(2048), f32(1024)],
        got,
    )


def multiply_kernel(left, right, back, held):
    total = None
    for core in range(2):
        lhs = jnp.concatenate([left[(2 * r + core) * 32 : (2 * r + core + 1) * 32, :] for r in range(8)])
        term = jnp.dot(right[core], lhs, preferred_element_type=jnp.float32)
        total = term if total is None else total + term
    total = total * FACTOR
    for half in range(2):
        for q in range(4):
            v = [total[(q * 4 + g) * 32 : (q * 4 + g + 1) * 32, half * 128 : (half + 1) * 128] for g in range(4)]
            for r, w in enumerate(swap(v)):
                for y in range(4):
                    held[chip_rows(half, r, y, q), :] = w[y * 8 : (y + 1) * 8, :]
    back[...] = held[...].reshape(256, 4, 128).astype(jnp.bfloat16)


def multiply(left, right):
    return call(
        multiply_kernel,
        jax.ShapeDtypeStruct((256, 4, 128), jnp.bfloat16),
        [f32(1024)],
        left, right,
    )


def unpack_kernel(mine, outgoing, incoming, held, rows, done, sems):
    copies = []
    for product, ref in ((0, outgoing), (1, incoming)):
        part = slice(product * 512, (product + 1) * 512)
        held[part, :] = mine[product * 128 : (product + 1) * 128].astype(jnp.float32).reshape(512, 128)
        for q in range(4):
            turned = held[pl.ds(product * 512 + q, 128, stride=4), :].T
            for g in range(4):
                rows[pl.ds(product * 512 + q * 4 + g, 32, stride=16), :] = turned[g * 32 : (g + 1) * 32, :]
        block = rows[product * 512 : (product + 1) * 512, :].astype(jnp.bfloat16)
        done[product] = block.reshape(32, 16, 128)
        copies.append(pltpu.make_async_copy(done.at[product], ref, sems.at[product]))
        copies[-1].start()
    for copy in copies:
        copy.wait()


def unpack(mine):
    return call(
        unpack_kernel,
        (jax.ShapeDtypeStruct((32, 16, 128), jnp.bfloat16),) * 2,
        [f32(1024), f32(1024), pltpu.VMEM((2, 32, 16, 128), jnp.bfloat16), pltpu.SemaphoreType.DMA((2,))],
        mine, out_space=pltpu.HBM,
    )


def body(out_left, out_right, in_left, in_right):
    got = lax.all_to_all(pack(out_left, out_right, in_left, in_right), CHIPS, 0, 0, tiled=True)
    left, right = sort(got)
    both = lax.all_gather(right, "core", axis=0, tiled=False)
    back = multiply(left, both)
    return unpack(lax.all_to_all(back, CHIPS, 0, 0, tiled=True))


def solution(mesh):
    fine = Mesh(mesh.devices.reshape(2, 4, 2, 4, 8), ROW + COL)
    in_specs = (P(ROW, COL, None), P(COL, ROW, None), P(COL, ROW, None), P(ROW, COL, None))
    out_specs = (P(ROW, COL, None), P(ROW, COL, None))
    return jax.shard_map(body, mesh=fine, in_specs=in_specs, out_specs=out_specs, check_vma=False)
```

```python
import math

import jax
import jax.numpy as jnp
from jax import lax
from jax.experimental import pallas as pl
from jax.experimental.pallas import tpu as pltpu
from jax.sharding import Mesh, PartitionSpec as P

ROW = ("y_lo", "x", "core")
COL = ("y_hi", "z")
CHIPS = ("y_hi", "y_lo", "z", "x")
STEP = {"y_hi": 64, "y_lo": 32, "z": 4, "x": 1}
FACTOR = 1.0 / math.sqrt(512)
MIB = 1024 * 1024


def call(kernel, shape, scratch, *args, space=pltpu.VMEM, out_space=pltpu.VMEM, limit=32):
    return pl.pallas_call(
        kernel,
        out_shape=shape,
        in_specs=[pl.BlockSpec(memory_space=space)] * len(args),
        out_specs=jax.tree.map(lambda _: pl.BlockSpec(memory_space=out_space), shape),
        scratch_shapes=scratch,
        compiler_params=pltpu.CompilerParams(vmem_limit_bytes=limit * MIB),
    )(*args)


def f32(rows):
    return pltpu.VMEM((rows, 128), jnp.float32)


def swap(v):
    lane = lax.broadcasted_iota(jnp.int32, v[0].shape, 1)
    even, low = (lane // 32) % 2 == 0, lane < 64
    middle = (lane >= 32) & (lane < 96)

    def pair(x, y):
        moved = pltpu.roll(jnp.where(even, y, x), 32, 1)
        return jnp.where(even, x, moved), jnp.where(even, moved, y)

    a0, a1 = pair(v[0], v[1])
    a2, a3 = pair(v[2], v[3])
    moved = pltpu.roll(jnp.where(low, a2, a0), 64, 1)
    w0, w2 = jnp.where(low, a0, moved), jnp.where(low, moved, a2)
    moved, kept = pltpu.roll(jnp.where(low, a3, a1), 64, 1), jnp.where(low, a1, a3)
    w1, w3 = jnp.where(middle, kept, moved), jnp.where(middle, moved, kept)
    return w0, w1, w2, w3


def pack_kernel(blocks, sent, rows, held):
    for n, product, side, a_first in ((0, 0, 0, True), (1, 0, 1, False), (2, 1, 0, False), (3, 1, 1, True)):
        block = blocks[n]
        if a_first:
            rows[...] = block.astype(jnp.float32)
            block = jnp.concatenate([rows[pl.ds(b, 32, stride=16), :] for b in range(16)])
            block = block.astype(jnp.bfloat16)
        turned = block.astype(jnp.float32).T
        for q in range(4):
            held[pl.ds(product * 1024 + side * 4 + q, 128, stride=8), :] = turned[:, q * 128 : (q + 1) * 128]
    sent[...] = held[...].astype(jnp.bfloat16).reshape(256, 8, 128)


def pack(*blocks):
    return call(
        pack_kernel,
        jax.ShapeDtypeStruct((256, 8, 128), jnp.bfloat16),
        [f32(512), f32(2048)],
        jnp.concatenate([block.reshape(512, 128) for block in blocks]).reshape(4, 512, 128),
    )


def chip_rows(half, r, y, q):
    first = half * STEP["y_lo"] + r * STEP["x"] + y * STEP["y_hi"]
    return pl.ds(first * 4 + q, 8, stride=STEP["z"] * 4)


def sort_kernel(got, left, right, got_f, sorted_f):
    tiles = got[...].astype(jnp.float32).reshape(64, 4, 8, 128)
    for r in range(4):
        got_f[r * 512 : (r + 1) * 512, :] = tiles[:, r].reshape(512, 128)
    for side in (1, 0):
        for half in range(2):
            lanes = slice(half * 128, (half + 1) * 128)
            for q in range(4):
                v = [
                    jnp.concatenate(
                        [got_f[pl.ds((r * 64 + y * 16 + half * 8) * 8 + side * 4 + q, 8, stride=8), :] for y in range(4)]
                    )
                    for r in range(4)
                ]
                for g, w in enumerate(swap(v)):
                    b = q * 4 + g
                    if side == 1:
                        right[b * 32 : (b + 1) * 32, lanes] = w.astype(jnp.bfloat16)
                    else:
                        sorted_f[pl.ds(half * 512 + b, 32, stride=16), :] = w
            if side == 0:
                left[:, lanes] = sorted_f[half * 512 : (half + 1) * 512, :].astype(jnp.bfloat16)


def sort(got):
    return call(
        sort_kernel,
        (jax.ShapeDtypeStruct((512, 256), jnp.bfloat16),) * 2,
        [f32(2048), f32(1024)],
        got,
    )


def multiply_kernel(left, right, back, held):
    blocks = [left[(2 * r + core) * 32 : (2 * r + core + 1) * 32, :] for core in range(2) for r in range(8)]
    rhs = jnp.concatenate([right[0], right[1]], axis=1)
    total = jnp.dot(rhs, jnp.concatenate(blocks), preferred_element_type=jnp.float32)
    total = total * FACTOR
    for half in range(2):
        for q in range(4):
            v = [total[(q * 4 + g) * 32 : (q * 4 + g + 1) * 32, half * 128 : (half + 1) * 128] for g in range(4)]
            for r, w in enumerate(swap(v)):
                for y in range(4):
                    held[chip_rows(half, r, y, q), :] = w[y * 8 : (y + 1) * 8, :]
    back[...] = held[...].reshape(256, 4, 128).astype(jnp.bfloat16)


def multiply(left, right):
    return call(
        multiply_kernel,
        jax.ShapeDtypeStruct((256, 4, 128), jnp.bfloat16),
        [f32(1024)],
        left, right,
    )


def unpack_kernel(mine, outgoing, incoming, held, rows, done, sems):
    copies = []
    for product, ref in ((0, outgoing), (1, incoming)):
        part = slice(product * 512, (product + 1) * 512)
        held[part, :] = mine[product * 128 : (product + 1) * 128].astype(jnp.float32).reshape(512, 128)
        for q in range(4):
            turned = held[pl.ds(product * 512 + q, 128, stride=4), :].T
            for g in range(4):
                rows[pl.ds(product * 512 + q * 4 + g, 32, stride=16), :] = turned[g * 32 : (g + 1) * 32, :]
        block = rows[product * 512 : (product + 1) * 512, :].astype(jnp.bfloat16)
        done[product] = block.reshape(32, 16, 128)
        copies.append(pltpu.make_async_copy(done.at[product], ref, sems.at[product]))
        copies[-1].start()
    for copy in copies:
        copy.wait()


def unpack(mine):
    return call(
        unpack_kernel,
        (jax.ShapeDtypeStruct((32, 16, 128), jnp.bfloat16),) * 2,
        [f32(1024), f32(1024), pltpu.VMEM((2, 32, 16, 128), jnp.bfloat16), pltpu.SemaphoreType.DMA((2,))],
        mine, out_space=pltpu.HBM,
    )


def body(out_left, out_right, in_left, in_right):
    got = lax.all_to_all(pack(out_left, out_right, in_left, in_right), CHIPS, 0, 0, tiled=True)
    left, right = sort(got)
    both = lax.all_gather(right, "core", axis=0, tiled=False)
    back = multiply(left, both)
    return unpack(lax.all_to_all(back, CHIPS, 0, 0, tiled=True))


def solution(mesh):
    fine = Mesh(mesh.devices.reshape(2, 4, 2, 4, 8), ROW + COL)
    in_specs = (P(ROW, COL, None), P(COL, ROW, None), P(COL, ROW, None), P(ROW, COL, None))
    out_specs = (P(ROW, COL, None), P(ROW, COL, None))
    return jax.shard_map(body, mesh=fine, in_specs=in_specs, out_specs=out_specs, check_vma=False)
```
